32 devices in a mesh: groups: 2 (over y), frames: 4 (over z), code: 2 (over x), head: 2 (over core).
Axes of the slice: x: 2, y: 2, z: 4, core: 2. Of those that a mesh axis runs over, the one named last changes fastest.
Arguments:
- video: bfloat16 [256, 16, 1024], P(('code', 'head'), ('groups', 'frames')), parts along dimension 1, may hold values from -6 to 6
- conv_weight: bfloat16 [3, 1024, 1024], replicated, may hold values from -0.109375 to 0.109375
- norm_gain: float32 [1024], replicated, may hold values from 0.1 to 1.9
- qkv_weight: bfloat16 [1024, 3, 1024], P(None, None, ('code', 'head')), may hold values from -1 to 1
- out_weight: bfloat16 [1024, 1024], P(('code', 'head')), may hold values from -0.1875 to 0.1875
- latent_weight: bfloat16 [1024, 16], replicated, may hold values from -0.1875 to 0.1875
- codebook: bfloat16 [16, 65536], P(None, ('code', 'head')), may hold values from -9 to 9
- reference_codes: int32 [256, 16], P(None, ('groups', 'frames')), parts along dimension 1, may hold values from 0 to 65535
Outputs:
- encoded: bfloat16 [256, 16, 1024], P(('code', 'head'), ('groups', 'frames')), parts along dimension 1
- nearest_distance: float32 [256, 16], P(('code', 'head'), ('groups', 'frames')), parts along dimension 1
- reference_gap: float32 [256, 16], P(('code', 'head'), ('groups', 'frames')), parts along dimension 1
The draws below stay inside these ranges and needn't reach their ends.
There are 2 independent parts, one for each index of `groups`. The reference program is written for one: setup_inputs(seed, part) draws one part's arguments, and reference() takes and returns one part's arrays. A program takes and returns all parts, laid end to end along the dimension named above; an argument that names none is the same for every part. Nothing has to cross between parts.
All inputs are finite; a program needn't handle non-finite values.
Results may differ from the reference program's by a relative error of at most 0.015.
Values may be sent and summed in bfloat16 or wider, within the bound.
A program may use at most 64 MiB of HBM per device.

```python
import math
import jax
import jax.numpy as jnp
from jax import lax

D = 1024
HEADS = 16
CODES = 65536
CDIM = 16
S = 256
F = 8


def draw_qkv_weight(key, part):
    first = jax.random.fold_in(jax.random.fold_in(key, 11), 0)
    base = jax.random.normal(first, (D, 3, D), jnp.float32) / math.sqrt(D)
    base = jnp.clip(base, -1.0, 1.0)
    return base.astype(jnp.bfloat16)


def with_ends(array, key, smallest, largest):
    dims = array.shape
    spot = [jax.random.randint(jax.random.fold_in(key, axis), (), 0, dims[axis]) for axis in range(len(dims))]
    array = array.at[tuple(spot)].set(smallest)
    longest = dims.index(max(dims))
    spot[longest] = (spot[longest] + 1) % dims[longest]
    return array.at[tuple(spot)].set(largest)


def block_scale(rng, dims, pieces, low, high):
    factor_of = 1.0
    for dim, parts in pieces:
        draws = jax.random.uniform(jax.random.fold_in(jax.random.fold_in(rng, 6), dim), (parts,), jnp.float32, low / len(pieces), high / len(pieces))
        factor_of = factor_of * jnp.repeat(jnp.exp(draws), dims[dim] // parts).reshape((-1,) + (1,) * (len(dims) - 1 - dim))
    return factor_of


def scatter_about(rng, extent, spread, most, pieces=(), kind=jnp.bfloat16):
    result = jax.random.normal(rng, extent, jnp.float32) * spread
    if len(pieces) > 0:
        result = block_scale(rng, extent, pieces, -0.22, 0.18) * result
    return jnp.clip(result, min=-most, max=most).astype(kind)


def setup_inputs(seed: int = 0, part: int = 0) -> dict:
    key_list = jax.random.split(jax.random.key(seed), 9)
    part_splits = jax.random.split(jax.random.fold_in(key_list[8], part), 9)
    return {
        "video": scatter_about(part_splits[0], (S, F, D), 1.0, 6.0, ((0, 4), (1, 4))),
        "conv_weight": scatter_about(key_list[1], (3, D, D), (3 * D) ** -0.5, 0.109375),
        "norm_gain": jnp.clip(1.0 + 0.18 * jax.random.normal(key_list[2], (D,), jnp.float32), 0.1, 1.9),
        "qkv_weight": draw_qkv_weight(jax.random.fold_in(key_list[8], 71), part),
        "out_weight": scatter_about(key_list[4], (D, D), D ** -0.5, 0.1875, ((0, 4),)),
        "latent_weight": scatter_about(key_list[5], (D, CDIM), D ** -0.5, 0.1875),
        "codebook": scatter_about(key_list[6], (CDIM, CODES), 1.5, 9.0, ((1, 4),)),
        "reference_codes": with_ends(jax.random.randint(part_splits[7], (S, F), 0, CODES), jax.random.fold_in(part_splits[7], 1), 0, CODES - 1).astype(jnp.int32),
    }


EPSILON = 1e-06

def conv_block(video, conv_weight):
    positions, frame_count, model_width = video.shape
    zeros_front = jnp.zeros((positions, 2, model_width), video.dtype)
    padded = jnp.concatenate([zeros_front, video], axis=1)
    stacked = jnp.concatenate([padded[:, 2:], padded[:, 1:-1], padded[:, :-2]], axis=2)
    mixed = jnp.dot(stacked.reshape(-1, 3 * model_width), conv_weight.reshape(3 * model_width, model_width), preferred_element_type=jnp.float32)
    return (video.reshape(-1, model_width).astype(jnp.float32) + jax.nn.silu(mixed)).astype(jnp.bfloat16)

def normalize(block_input, norm_gain):
    values32 = block_input.astype(jnp.float32)
    mean_square = lax.optimization_barrier(jnp.mean(values32 * values32, axis=-1, keepdims=True))
    return (values32 * lax.rsqrt(mean_square + EPSILON) * norm_gain).astype(jnp.bfloat16)

def attend(queries, keys, values, frame_of):
    head_count, token_count, head_dim = queries.shape
    block = math.gcd(token_count, 1024)
    score_scale = 1.0 / math.sqrt(head_dim)

    def one_head(operands):
        head_q, head_k, head_v = operands

        def one_block(block_index):
            rows_q = lax.dynamic_slice_in_dim(head_q, block_index * block, block, 0)
            frames_q = lax.dynamic_slice_in_dim(frame_of, block_index * block, block, 0)
            scores = jnp.dot(rows_q, head_k.T, preferred_element_type=jnp.float32) * score_scale
            allowed = frame_of[None, :] <= frames_q[:, None]
            highest = lax.optimization_barrier(jnp.max(jnp.where(allowed, scores, -1e+30), axis=1, keepdims=True))
            weights = jnp.where(allowed, jnp.exp(scores - highest), 0.0)
            denominator = lax.optimization_barrier(jnp.sum(weights, axis=1, keepdims=True))
            return jnp.dot(weights.astype(jnp.bfloat16), head_v, preferred_element_type=jnp.float32) / denominator
        blocks = lax.map(one_block, jnp.arange(token_count // block, dtype=jnp.int32))
        return blocks.reshape(token_count, head_dim).astype(jnp.bfloat16)
    return lax.map(one_head, (queries, keys, values))

def search(latent, codebook, reference_codes):
    code_dim, code_count = codebook.shape
    block = math.gcd(code_count, 4096)
    latent32 = latent.astype(jnp.float32)
    squares = lax.optimization_barrier(jnp.sum(latent32 * latent32, axis=1))
    wanted = reference_codes.reshape(-1)

    def visit(running, block_index):
        least, chosen = running
        codes = lax.dynamic_slice_in_dim(codebook, block_index * block, block, 1)
        codes32 = codes.astype(jnp.float32)
        code_squares = lax.optimization_barrier(jnp.sum(codes32 * codes32, axis=0))
        dots = jnp.dot(latent, codes, preferred_element_type=jnp.float32)
        distance = (squares[:, None] - 2.0 * dots + code_squares[None, :]) / code_dim
        labels = block_index * block + jnp.arange(block, dtype=jnp.int32)
        least = jnp.minimum(least, lax.optimization_barrier(jnp.min(distance, axis=1)))
        chosen = chosen + lax.optimization_barrier(jnp.sum(jnp.where(labels[None, :] == wanted[:, None], distance, 0.0), axis=1))
        return ((least, chosen), None)
    start_state = (jnp.full(squares.shape, 1e+30, jnp.float32), jnp.zeros(squares.shape, jnp.float32))
    (least, chosen), unused = lax.scan(visit, start_state, jnp.arange(code_count // block, dtype=jnp.int32))
    return (least, chosen)

def reference(video, conv_weight, norm_gain, qkv_weight, out_weight, latent_weight, codebook, reference_codes):
    positions, frame_count, model_width = video.shape
    token_count = positions * frame_count
    head_dim = model_width // HEADS
    block_input = conv_block(video, conv_weight)
    normed = normalize(block_input, norm_gain)
    triple = jnp.dot(normed, qkv_weight.reshape(model_width, 3 * model_width), preferred_element_type=jnp.float32).astype(jnp.bfloat16)
    triple = triple.reshape(token_count, 3, HEADS, head_dim)
    queries = jnp.transpose(triple[:, 0], (1, 0, 2))
    keys = jnp.transpose(triple[:, 1], (1, 0, 2))
    values = jnp.transpose(triple[:, 2], (1, 0, 2))
    frame_of = jnp.arange(token_count, dtype=jnp.int32) % frame_count
    heads_out = attend(queries, keys, values, frame_of)
    attended = jnp.transpose(heads_out, (1, 0, 2)).reshape(token_count, model_width)
    projected = jnp.dot(attended, out_weight, preferred_element_type=jnp.float32)
    encoded = (block_input.astype(jnp.float32) + projected).astype(jnp.bfloat16)
    latent = jnp.dot(encoded, latent_weight, preferred_element_type=jnp.float32).astype(jnp.bfloat16)
    least, chosen = search(latent, codebook, reference_codes)
    return (encoded.reshape(positions, frame_count, model_width), least.reshape(positions, frame_count), (chosen - least).reshape(positions, frame_count))
```

```python
import functools
import math

import jax
import jax.numpy as jnp
from jax import lax
from jax.experimental import pallas as pl
from jax.experimental.pallas import tpu as pltpu
from jax.sharding import PartitionSpec as P

HEADS = 16
EPSILON = 1e-06
LANES = 128
MESH = pl.DeviceIdType.MESH
BF16 = jnp.bfloat16
F32 = jnp.float32


def tile_of(length, most):
    return math.gcd(length, most)


def encoder_kernel(
    n_f, n_c, n_h,
    video_ref, conv_w_hbm, gain_ref, qkv_w_hbm, out_w_hbm, latent_w_ref, codes_hbm, wanted_ref,
    encoded_ref, least_ref, gap_ref,
    ext, conv_w, mixed, block_input, normed, qkv_w, queries, kv, top, denom, summed,
    attended, gathered, out_w, codes, augmented, lhs, wanted,
    local_sems, send_sems, recv_sems, kv_send, kv_recv, halo_send, halo_recv,
):
    n_g = n_c * n_h
    fr = lax.axis_index("frames")
    c = lax.axis_index("code")
    h = lax.axis_index("head")
    g = c * n_h + h
    fh, pos, width = video_ref.shape
    rows = fh * pos
    chip_rows = n_h * rows
    lw = out_w_hbm.shape[0]
    pairs = lw // LANES
    head_dim = width // HEADS
    per_tile = LANES // head_dim
    slab = n_g * rows
    code_dim, shard = codes_hbm.shape

    def device(c2, h2):
        return {"code": c2, "head": h2}

    conv_copies = [
        pltpu.make_async_copy(conv_w_hbm.at[k], conv_w.at[k], local_sems.at[k]) for k in range(3)
    ]
    qkv_copy = pltpu.make_async_copy(qkv_w_hbm, qkv_w, local_sems.at[3])
    out_copy = pltpu.make_async_copy(out_w_hbm, out_w.at[g], local_sems.at[4])
    codes_copy = pltpu.make_async_copy(codes_hbm, codes.at[g], local_sems.at[5])
    for copy in [codes_copy] + conv_copies + [qkv_copy, out_copy]:
        copy.start()

    barrier = pltpu.get_barrier_semaphore()
    for dc in range(n_c):
        for dh in range(n_h):
            if dc or dh:
                pl.semaphore_signal(
                    barrier, inc=1,
                    device_id=device(lax.rem(c + dc, n_c), lax.rem(h + dh, n_h)),
                    device_id_type=MESH,
                )
    for df in range(1, n_f):
        pl.semaphore_signal(
            barrier, inc=1, device_id={"frames": lax.rem(fr + df, n_f)}, device_id_type=MESH
        )
    pl.semaphore_wait(barrier, n_g - 1 + n_f - 1)

    halo = pltpu.make_async_remote_copy(
        src_ref=video_ref.at[pl.ds(fh - 2, 2)],
        dst_ref=ext.at[pl.ds(0, 2)],
        send_sem=halo_send,
        recv_sem=halo_recv,
        device_id={"frames": lax.rem(fr + 1, n_f)},
        device_id_type=MESH,
    )

    @pl.when(fr + 1 < n_f)
    def _():
        halo.start()

    started = []

    def send(kind, block, slot, c2, h2):
        copy = pltpu.make_async_remote_copy(
            src_ref=block(slot),
            dst_ref=block(slot),
            send_sem=send_sems.at[len(started)],
            recv_sem=recv_sems.at[kind, slot],
            device_id=device(c2, h2),
            device_id_type=MESH,
        )
        copy.start()
        started.append(copy)

    def arrived(kind, block, slot):
        pltpu.make_async_remote_copy(
            src_ref=block(slot),
            dst_ref=block(slot),
            send_sem=send_sems.at[0],
            recv_sem=recv_sems.at[kind, slot],
            device_id=device(c, lax.rem(h + 1, n_h)),
            device_id_type=MESH,
        ).wait_recv()

    def slot_of(dc, dh):
        return lax.rem(c + n_c - dc, n_c) * n_h + lax.rem(h + n_h - dh, n_h)

    def spread(kind, block):
        for dc in range(1, n_c):
            send(kind, block, g, lax.rem(c + dc, n_c), h)
        for dh in range(1, n_h):
            send(kind, block, g, c, lax.rem(h + dh, n_h))

    def forward(kind, block, dc):
        slot = slot_of(dc, 0)
        arrived(kind, block, slot)
        for dh in range(1, n_h):
            send(kind, block, slot, c, lax.rem(h + dh, n_h))

    def rest(kind, block, dc):
        for dh in range(1, n_h):
            arrived(kind, block, slot_of(dc, dh))

    def codes_block(slot):
        return codes.at[slot]

    def normed_block(slot):
        return normed.at[pl.ds(pl.multiple_of(slot * rows, rows), rows)]

    def out_block(slot):
        return out_w.at[slot]

    codes_copy.wait()
    spread(0, codes_block)

    ext[2:] = video_ref[...]
    tile = tile_of(width, 256)

    def tap(k):
        conv_copies[k].wait()
        taken = ext[2 - k : 2 - k + fh].reshape(rows, width)

        @pl.loop(0, width // tile)
        def _(n):
            cols = pl.ds(pl.multiple_of(n * tile, tile), tile)
            part = jnp.dot(taken, conv_w[k, :, cols], preferred_element_type=F32)
            if k == 0:
                mixed[:, cols] = part
            else:
                mixed[:, cols] = mixed[:, cols] + part

    tap(0)

    @pl.when(fr > 0)
    def _():
        halo.wait_recv()

    @pl.when(fr == 0)
    def _():
        ext[:2] = jnp.zeros((2, pos, width), BF16)

    tap(1)
    tap(2)
    conv = mixed[...]
    values = (video_ref[...].reshape(rows, width).astype(F32) + conv / (1.0 + jnp.exp(-conv))).astype(BF16)
    block_input[...] = values
    values32 = values.astype(F32)
    mean_square = jnp.mean(values32 * values32, axis=-1, keepdims=True)
    normed[pl.ds(pl.multiple_of(g * rows, rows), rows), :] = (
        values32 * lax.rsqrt(mean_square + EPSILON) * gain_ref[...]
    ).astype(BF16)
    spread(1, normed_block)

    def project(c2):
        at = pl.ds(pl.multiple_of(c2 * chip_rows, chip_rows), chip_rows)
        taken = normed[at, :]
        for kind in range(3):
            out = jnp.dot(taken, qkv_w[kind], preferred_element_type=F32)
            out = out.astype(BF16)
            for p in range(pairs):
                piece = out[:, p * LANES : (p + 1) * LANES]
                if kind == 0:
                    queries[p, at, :] = piece * (1.0 / math.sqrt(head_dim))
                else:
                    kv[fr, kind - 1, p, at, :] = piece

    qkv_copy.wait()
    rest(1, normed_block, 0)
    project(c)
    for dc in range(1, n_c):
        forward(1, normed_block, dc)
    out_copy.wait()
    spread(2, out_block)
    for dc in range(1, n_c):
        rest(1, normed_block, dc)
        project(lax.rem(c + n_c - dc, n_c))

    def kv_copy(slot, df):
        return pltpu.make_async_remote_copy(
            src_ref=kv.at[slot],
            dst_ref=kv.at[slot],
            send_sem=kv_send.at[df],
            recv_sem=kv_recv.at[slot],
            device_id={"frames": lax.rem(fr + df, n_f)},
            device_id_type=MESH,
        )

    for df in range(1, n_f):
        @pl.when(fr + df < n_f)
        def _():
            kv_copy(fr, df).start()

    q_tile = tile_of(slab, 256)
    lane = lax.broadcasted_iota(jnp.int32, (q_tile, LANES), 1) // head_dim

    def by_head(parts):
        out = parts[0]
        for k in range(1, per_tile):
            out = jnp.where(lane == k, parts[k], out)
        return out

    def absorb(slot, own):
        @pl.loop(0, pairs * (slab // q_tile))
        def _(step):
            p = step // (slab // q_tile)
            first = (step % (slab // q_tile)) * q_tile
            at = pl.ds(pl.multiple_of(first, q_tile), q_tile)
            q = queries[p, at, :]
            k = kv[slot, 0, p]
            v = kv[slot, 1, p]
            if own:
                q_row = first + lax.broadcasted_iota(jnp.int32, (q_tile, slab), 0)
                k_row = lax.broadcasted_iota(jnp.int32, (q_tile, slab), 1)
                allowed = (k_row // pos) % fh <= (q_row // pos) % fh
            else:
                old_top = top[p, at, :]
            tops, factors, sums, outs = [], [], [], []
            for hh in range(per_tile):
                mine = jnp.where(lane == hh, q, jnp.zeros_like(q))
                scores = lax.dot_general(mine, k, (((1,), (1,)), ((), ())), preferred_element_type=F32)
                if own:
                    scores = jnp.where(allowed, scores, -1e30)
                fresh = jnp.max(scores, axis=1, keepdims=True)
                if not own:
                    old = old_top[:, hh * head_dim : hh * head_dim + 1]
                    fresh = jnp.maximum(fresh, old)
                    factors.append(jnp.exp(old - fresh))
                weights = jnp.exp(scores - fresh)
                tops.append(fresh)
                sums.append(jnp.sum(weights, axis=1, keepdims=True))
                outs.append(jnp.dot(weights.astype(BF16), v, preferred_element_type=F32))
            top[p, at, :] = by_head([jnp.broadcast_to(x, (q_tile, LANES)) for x in tops])
            total = by_head([jnp.broadcast_to(x, (q_tile, LANES)) for x in sums])
            out = by_head(outs)
            if own:
                denom[p, at, :] = total
                summed[p, at, :] = out
            else:
                factor = by_head([jnp.broadcast_to(x, (q_tile, LANES)) for x in factors])
                denom[p, at, :] = denom[p, at, :] * factor + total
                summed[p, at, :] = summed[p, at, :] * factor + out

    absorb(fr, True)

    for dc in range(1, n_c):
        forward(0, codes_block, dc)
    for dc in range(n_c):
        rest(0, codes_block, dc)
    c_tile = tile_of(shard, 1024)

    @pl.loop(0, n_g * (shard // c_tile))
    def _(step):
        slot = step // (shard // c_tile)
        cols = pl.ds(pl.multiple_of((step % (shard // c_tile)) * c_tile, c_tile), c_tile)
        block = codes[slot, :, cols]
        block32 = block.astype(F32)
        squares = jnp.sum(block32 * block32, axis=0, keepdims=True)
        high = squares.astype(BF16).astype(F32)
        middle = (squares - high).astype(BF16).astype(F32)
        low = squares - high - middle
        row = lax.broadcasted_iota(jnp.int32, (code_dim, c_tile), 0)
        extra = jnp.where(row == 0, high, jnp.where(row == 1, middle, jnp.where(row == 2, low, 0.0)))
        augmented[slot, :code_dim, cols] = block
        augmented[slot, code_dim:, cols] = extra.astype(BF16)

    for dc in range(1, n_c):
        forward(2, out_block, dc)
    for dc in range(n_c):
        rest(2, out_block, dc)

    def visit(k, carry):
        slot = fr - 1 - k
        kv_copy(slot, 1).wait_recv()
        absorb(slot, False)
        return carry

    lax.fori_loop(0, fr, visit, 0)

    for p in range(pairs):
        attended[:, p * LANES : (p + 1) * LANES] = (summed[p] / denom[p]).astype(BF16)

    def rows_at(slot):
        return pl.ds(pl.multiple_of(slot * rows, rows), rows)

    def exchange(dc, dh):
        c2, h2 = lax.rem(c + dc, n_c), lax.rem(h + dh, n_h)
        copy = pltpu.make_async_remote_copy(
            src_ref=attended.at[rows_at(c2 * n_h + h2)],
            dst_ref=gathered.at[g],
            send_sem=send_sems.at[len(started)],
            recv_sem=recv_sems.at[3, g],
            device_id=device(c2, h2),
            device_id_type=MESH,
        )
        copy.start()
        started.append(copy)

    order = [(dc, dh) for dc in range(n_c) for dh in range(n_h) if dc or dh]
    for dc, dh in reversed(order):
        exchange(dc, dh)

    def project_out(taken, slot, fresh):
        @pl.loop(0, width // tile)
        def _(n):
            cols = pl.ds(pl.multiple_of(n * tile, tile), tile)
            part = jnp.dot(taken, out_w[slot, :, cols], preferred_element_type=F32)
            if fresh:
                mixed[:, cols] = part
            else:
                mixed[:, cols] = mixed[:, cols] + part

    project_out(attended[rows_at(g), :], g, True)
    for dc, dh in order:
        slot = slot_of(dc, dh)
        arrived(3, lambda s: gathered.at[s], slot)
        project_out(gathered[slot], slot, False)

    encoded = (block_input[...].astype(F32) + mixed[...]).astype(BF16)
    encoded_ref[...] = encoded.reshape(fh, pos, width)
    latent = lax.dot_general(
        encoded, latent_w_ref[...], (((1,), (1,)), ((), ())), preferred_element_type=F32
    ).astype(BF16).astype(F32)
    square = jnp.sum(latent * latent, axis=1, keepdims=True)
    column = lax.broadcasted_iota(jnp.int32, lhs.shape, 1)
    lhs[...] = jnp.where(column < code_dim + 3, 1.0, 0.0)
    lhs[:, :code_dim] = -2.0 * latent
    left = lhs[...].astype(BF16)

    everyone = (pos, wanted_ref.shape[1])
    is_mine = lax.broadcasted_iota(jnp.int32, everyone, 0) + g * pos == lax.broadcasted_iota(
        jnp.int32, everyone, 1
    )
    for t in range(fh):
        mine = jnp.where(is_mine, jnp.broadcast_to(wanted_ref[t : t + 1, :], everyone), 0)
        wanted[t * pos : (t + 1) * pos, :] = jnp.broadcast_to(
            jnp.sum(mine, axis=1, keepdims=True), (pos, LANES)
        )
    lanes = lax.broadcasted_iota(jnp.int32, (1, LANES), 1)

    def search(step, state):
        least, chosen = state
        slot = step // (shard // c_tile)
        cols = pl.ds(pl.multiple_of((step % (shard // c_tile)) * c_tile, c_tile), c_tile)
        found = jnp.dot(left, augmented[slot, :, cols], preferred_element_type=F32)
        sought = wanted[...]
        for k in range(c_tile // LANES):
            part = found[:, k * LANES : (k + 1) * LANES]
            labels = lanes + (step * c_tile + k * LANES)
            least = jnp.minimum(least, part)
            chosen = jnp.where(sought == labels, part, chosen)
        return least, chosen

    least, chosen = lax.fori_loop(
        0, n_g * (shard // c_tile), search,
        (jnp.full((rows, LANES), 3e38, F32), jnp.zeros((rows, LANES), F32)),
    )
    least = (jnp.min(least, axis=1, keepdims=True) + square) / code_dim
    chosen = (jnp.sum(chosen, axis=1, keepdims=True) + square) / code_dim
    gap = chosen - least
    diagonal = lax.broadcasted_iota(jnp.int32, (pos, pos), 0) == lax.broadcasted_iota(
        jnp.int32, (pos, pos), 1
    )
    for t in range(fh):
        for ref, column in ((least_ref, least), (gap_ref, gap)):
            square_part = jnp.broadcast_to(column[t * pos : (t + 1) * pos], (pos, pos))
            ref[t : t + 1, :] = jnp.sum(
                jnp.where(diagonal, square_part, 0.0), axis=0, keepdims=True
            )

    for copy in started:
        copy.wait_send()

    @pl.when(fr + 1 < n_f)
    def _():
        halo.wait_send()

    for df in range(1, n_f):
        @pl.when(fr + df < n_f)
        def _():
            kv_copy(fr, df).wait_send()


def shards(
    n_f, n_c, n_h,
    video, conv_weight, norm_gain, qkv_weight, out_weight, latent_weight, codebook, reference_codes,
):
    positions, frames_here, width = video.shape
    rows = positions * frames_here
    n_g = n_c * n_h
    slab = n_g * rows
    lw = qkv_weight.shape[2]
    pairs = lw // LANES
    code_dim, shard = codebook.shape
    sends = 3 * (n_c - 1 + n_h - 1 + (n_c - 1) * (n_h - 1)) + n_g - 1
    vmem = pl.BlockSpec(memory_space=pltpu.VMEM)
    anywhere = pl.BlockSpec(memory_space=pl.ANY)
    encoded, least, gap = pl.pallas_call(
        functools.partial(encoder_kernel, n_f, n_c, n_h),
        out_shape=(
            jax.ShapeDtypeStruct((frames_here, positions, width), BF16),
            jax.ShapeDtypeStruct((frames_here, positions), F32),
            jax.ShapeDtypeStruct((frames_here, positions), F32),
        ),
        in_specs=[vmem, anywhere, vmem, anywhere, anywhere, vmem, anywhere, vmem],
        out_specs=(vmem, vmem, vmem),
        scratch_shapes=[
            pltpu.VMEM((2 + frames_here, positions, width), BF16),
            pltpu.VMEM(conv_weight.shape, BF16),
            pltpu.VMEM((rows, width), F32),
            pltpu.VMEM((rows, width), BF16),
            pltpu.VMEM((slab, width), BF16),
            pltpu.VMEM((3, width, lw), BF16),
            pltpu.VMEM((pairs, slab, LANES), BF16),
            pltpu.VMEM((n_f, 2, pairs, slab, LANES), BF16),
            pltpu.VMEM((pairs, slab, LANES), F32),
            pltpu.VMEM((pairs, slab, LANES), F32),
            pltpu.VMEM((pairs, slab, LANES), F32),
            pltpu.VMEM((slab, lw), BF16),
            pltpu.VMEM((n_g, rows, lw), BF16),
            pltpu.VMEM((n_g, lw, width), BF16),
            pltpu.VMEM((n_g, code_dim, shard), BF16),
            pltpu.VMEM((n_g, 2 * code_dim, shard), BF16),
            pltpu.VMEM((rows, 2 * code_dim), F32),
            pltpu.VMEM((rows, LANES), jnp.int32),
            pltpu.SemaphoreType.DMA((6,)),
            pltpu.SemaphoreType.DMA((sends,)),
            pltpu.SemaphoreType.DMA((4, n_g)),
            pltpu.SemaphoreType.DMA((n_f,)),
            pltpu.SemaphoreType.DMA((n_f,)),
            pltpu.SemaphoreType.DMA,
            pltpu.SemaphoreType.DMA,
        ],
        compiler_params=pltpu.CompilerParams(
            collective_id=0, has_side_effects=True, vmem_limit_bytes=48 * 1024 * 1024
        ),
    )(
        jnp.transpose(video, (1, 0, 2)),
        conv_weight,
        norm_gain.reshape(1, width),
        jnp.transpose(qkv_weight, (1, 0, 2)),
        out_weight,
        jnp.transpose(latent_weight),
        codebook,
        jnp.transpose(reference_codes),
    )
    return jnp.transpose(encoded, (1, 0, 2)), jnp.transpose(least), jnp.transpose(gap)


def solution(mesh):
    sizes = [mesh.shape[axis] for axis in ("frames", "code", "head")]
    return jax.shard_map(
        functools.partial(shards, *sizes),
        mesh=mesh,
        in_specs=(
            P(("code", "head"), ("groups", "frames"), None),
            P(),
            P(),
            P(None, None, ("code", "head")),
            P(("code", "head"), None),
            P(),
            P(None, ("code", "head")),
            P(None, ("groups", "frames")),
        ),
        out_specs=(
            P(("code", "head"), ("groups", "frames"), None),
            P(("code", "head"), ("groups", "frames")),
            P(("code", "head"), ("groups", "frames")),
        ),
        check_vma=False,
    )
```

```python
import functools
import math

import jax
import jax.numpy as jnp
from jax import lax
from jax.experimental import pallas as pl
from jax.experimental.pallas import tpu as pltpu
from jax.sharding import PartitionSpec as P

HEADS = 16
EPSILON = 1e-06
LANES = 128
MESH = pl.DeviceIdType.MESH
BF16 = jnp.bfloat16
F32 = jnp.float32


def tile_of(length, most):
    return math.gcd(length, most)


def encoder_kernel(
    n_f, n_c, n_h,
    video_hbm, conv_w_hbm, gain_hbm, qkv_w_hbm, out_w_hbm, latent_w_hbm, codes_hbm, wanted_hbm,
    encoded_ref, least_ref, gap_ref,
    gain_ref, latent_w_ref, wanted_ref, ext, conv_w, mixed, block_input, normed, qkv_w, queries, kv, top, denom, summed,
    attended, gathered, out_w, codes, augmented, lhs, wanted,
    local_sems, send_sems, recv_sems, kv_send, kv_recv, halo_send, halo_recv,
):
    n_g = n_c * n_h
    fr = lax.axis_index("frames")
    c = lax.axis_index("code")
    h = lax.axis_index("head")
    g = c * n_h + h
    fh, pos, width = video_hbm.shape
    rows = fh * pos
    chip_rows = n_h * rows
    lw = out_w_hbm.shape[0]
    pairs = lw // LANES
    head_dim = width // HEADS
    per_tile = LANES // head_dim
    slab = n_g * rows
    code_dim, shard = codes_hbm.shape

    def device(c2, h2):
        return {"code": c2, "head": h2}

    conv_copies = [
        pltpu.make_async_copy(conv_w_hbm.at[k], conv_w.at[k], local_sems.at[k]) for k in range(3)
    ]
    qkv_copy = pltpu.make_async_copy(qkv_w_hbm, qkv_w, local_sems.at[3])
    out_copy = pltpu.make_async_copy(out_w_hbm, out_w.at[g], local_sems.at[4])
    codes_copy = pltpu.make_async_copy(codes_hbm, codes.at[g], local_sems.at[5])
    video_copy = pltpu.make_async_copy(video_hbm, ext.at[pl.ds(2, fh)], local_sems.at[6])
    gain_copy = pltpu.make_async_copy(gain_hbm, gain_ref, local_sems.at[7])
    latent_w_copy = pltpu.make_async_copy(latent_w_hbm, latent_w_ref, local_sems.at[8])
    wanted_copy = pltpu.make_async_copy(wanted_hbm, wanted_ref, local_sems.at[9])
    small_copies = [gain_copy, latent_w_copy, wanted_copy]
    for copy in [codes_copy, video_copy] + conv_copies + [qkv_copy, out_copy] + small_copies:
        copy.start()

    barrier = pltpu.get_barrier_semaphore()
    for dc in range(n_c):
        for dh in range(n_h):
            if dc or dh:
                pl.semaphore_signal(
                    barrier, inc=1,
                    device_id=device(lax.rem(c + dc, n_c), lax.rem(h + dh, n_h)),
                    device_id_type=MESH,
                )
    for df in range(1, n_f):
        pl.semaphore_signal(
            barrier, inc=1, device_id={"frames": lax.rem(fr + df, n_f)}, device_id_type=MESH
        )
    pl.semaphore_wait(barrier, n_g - 1 + n_f - 1)

    halo = pltpu.make_async_remote_copy(
        src_ref=video_hbm.at[pl.ds(fh - 2, 2)],
        dst_ref=ext.at[pl.ds(0, 2)],
        send_sem=halo_send,
        recv_sem=halo_recv,
        device_id={"frames": lax.rem(fr + 1, n_f)},
        device_id_type=MESH,
    )

    @pl.when(fr + 1 < n_f)
    def _():
        halo.start()

    started = []

    def send(kind, block, slot, c2, h2):
        copy = pltpu.make_async_remote_copy(
            src_ref=block(slot),
            dst_ref=block(slot),
            send_sem=send_sems.at[len(started)],
            recv_sem=recv_sems.at[kind, slot],
            device_id=device(c2, h2),
            device_id_type=MESH,
        )
        copy.start()
        started.append(copy)

    def arrived(kind, block, slot):
        pltpu.make_async_remote_copy(
            src_ref=block(slot),
            dst_ref=block(slot),
            send_sem=send_sems.at[0],
            recv_sem=recv_sems.at[kind, slot],
            device_id=device(c, lax.rem(h + 1, n_h)),
            device_id_type=MESH,
        ).wait_recv()

    def slot_of(dc, dh):
        return lax.rem(c + n_c - dc, n_c) * n_h + lax.rem(h + n_h - dh, n_h)

    def spread(kind, block):
        for dc in range(1, n_c):
            send(kind, block, g, lax.rem(c + dc, n_c), h)
        for dh in range(1, n_h):
            send(kind, block, g, c, lax.rem(h + dh, n_h))

    def forward(kind, block, dc):
        slot = slot_of(dc, 0)
        arrived(kind, block, slot)
        for dh in range(1, n_h):
            send(kind, block, slot, c, lax.rem(h + dh, n_h))

    def rest(kind, block, dc):
        for dh in range(1, n_h):
            arrived(kind, block, slot_of(dc, dh))

    def codes_block(slot):
        return codes.at[slot]

    def normed_block(slot):
        return normed.at[pl.ds(pl.multiple_of(slot * rows, rows), rows)]

    def out_block(slot):
        return out_w.at[slot]

    codes_copy.wait()
    spread(0, codes_block)

    video_copy.wait()
    tile = tile_of(width, 256)

    def tap(k):
        conv_copies[k].wait()
        taken = ext[2 - k : 2 - k + fh].reshape(rows, width)

        @pl.loop(0, width // tile)
        def _(n):
            cols = pl.ds(pl.multiple_of(n * tile, tile), tile)
            part = jnp.dot(taken, conv_w[k, :, cols], preferred_element_type=F32)
            if k == 0:
                mixed[:, cols] = part
            else:
                mixed[:, cols] = mixed[:, cols] + part

    tap(0)

    @pl.when(fr > 0)
    def _():
        halo.wait_recv()

    @pl.when(fr == 0)
    def _():
        ext[:2] = jnp.zeros((2, pos, width), BF16)

    tap(1)
    tap(2)
    for copy in small_copies:
        copy.wait()
    conv = mixed[...]
    values = (ext[2:].reshape(rows, width).astype(F32) + conv / (1.0 + jnp.exp(-conv))).astype(BF16)
    block_input[...] = values
    values32 = values.astype(F32)
    mean_square = jnp.mean(values32 * values32, axis=-1, keepdims=True)
    normed[pl.ds(pl.multiple_of(g * rows, rows), rows), :] = (
        values32 * lax.rsqrt(mean_square + EPSILON) * gain_ref[...]
    ).astype(BF16)
    spread(1, normed_block)

    def project(c2):
        at = pl.ds(pl.multiple_of(c2 * chip_rows, chip_rows), chip_rows)
        taken = normed[at, :]
        for kind in range(3):
            out = jnp.dot(taken, qkv_w[kind], preferred_element_type=F32)
            out = out.astype(BF16)
            for p in range(pairs):
                piece = out[:, p * LANES : (p + 1) * LANES]
                if kind == 0:
                    queries[p, at, :] = piece * (1.0 / math.sqrt(head_dim))
                else:
                    kv[fr, c2, kind - 1, p] = piece

    def kv_copy(slot, c2, df):
        return pltpu.make_async_remote_copy(
            src_ref=kv.at[slot, c2],
            dst_ref=kv.at[slot, c2],
            send_sem=kv_send.at[df, c2],
            recv_sem=kv_recv.at[slot, c2],
            device_id={"frames": lax.rem(fr + df, n_f)},
            device_id_type=MESH,
        )

    def send_kv(c2):
        for df in reversed(range(1, n_f)):
            @pl.when(fr + df < n_f)
            def _():
                kv_copy(fr, c2, df).start()

    qkv_copy.wait()
    rest(1, normed_block, 0)
    project(c)
    send_kv(c)
    for dc in range(1, n_c):
        forward(1, normed_block, dc)
    out_copy.wait()
    spread(2, out_block)
    for dc in range(1, n_c):
        rest(1, normed_block, dc)
        other = lax.rem(c + n_c - dc, n_c)
        project(other)
        send_kv(other)

    q_tile = tile_of(slab, 256)
    lane = lax.broadcasted_iota(jnp.int32, (q_tile, LANES), 1) // head_dim

    def by_head(parts):
        out = parts[0]
        for k in range(1, per_tile):
            out = jnp.where(lane == k, parts[k], out)
        return out

    def absorb(slot, own):
        @pl.loop(0, pairs * (slab // q_tile))
        def _(step):
            p = step // (slab // q_tile)
            first = (step % (slab // q_tile)) * q_tile
            at = pl.ds(pl.multiple_of(first, q_tile), q_tile)
            q = queries[p, at, :]
            k = kv[slot, :, 0, p].reshape(slab, LANES)
            v = kv[slot, :, 1, p].reshape(slab, LANES)
            if own:
                q_row = first + lax.broadcasted_iota(jnp.int32, (q_tile, slab), 0)
                k_row = lax.broadcasted_iota(jnp.int32, (q_tile, slab), 1)
                allowed = (k_row // pos) % fh <= (q_row // pos) % fh
            else:
                old_top = top[p, at, :]
            tops, factors, sums, outs = [], [], [], []
            for hh in range(per_tile):
                mine = jnp.where(lane == hh, q, jnp.zeros_like(q))
                scores = lax.dot_general(mine, k, (((1,), (1,)), ((), ())), preferred_element_type=F32)
                if own:
                    scores = jnp.where(allowed, scores, -1e30)
                fresh = jnp.max(scores, axis=1, keepdims=True)
                if not own:
                    old = old_top[:, hh * head_dim : hh * head_dim + 1]
                    fresh = jnp.maximum(fresh, old)
                    factors.append(jnp.exp(old - fresh))
                weights = jnp.exp(scores - fresh)
                tops.append(fresh)
                sums.append(jnp.sum(weights, axis=1, keepdims=True))
                outs.append(jnp.dot(weights.astype(BF16), v, preferred_element_type=F32))
            top[p, at, :] = by_head([jnp.broadcast_to(x, (q_tile, LANES)) for x in tops])
            total = by_head([jnp.broadcast_to(x, (q_tile, LANES)) for x in sums])
            out = by_head(outs)
            if own:
                denom[p, at, :] = total
                summed[p, at, :] = out
            else:
                factor = by_head([jnp.broadcast_to(x, (q_tile, LANES)) for x in factors])
                denom[p, at, :] = denom[p, at, :] * factor + total
                summed[p, at, :] = summed[p, at, :] * factor + out

    absorb(fr, True)

    for dc in range(1, n_c):
        forward(0, codes_block, dc)
    for dc in range(n_c):
        rest(0, codes_block, dc)
    c_tile = tile_of(shard, 8192)

    @pl.loop(0, n_g * (shard // c_tile))
    def _(step):
        slot = step // (shard // c_tile)
        cols = pl.ds(pl.multiple_of((step % (shard // c_tile)) * c_tile, c_tile), c_tile)
        block = codes[slot, :, cols]
        block32 = block.astype(F32)
        squares = jnp.sum(block32 * block32, axis=0, keepdims=True)
        high = squares.astype(BF16).astype(F32)
        middle = (squares - high).astype(BF16).astype(F32)
        low = squares - high - middle
        row = lax.broadcasted_iota(jnp.int32, (code_dim, c_tile), 0)
        extra = jnp.where(row == 0, high, jnp.where(row == 1, middle, jnp.where(row == 2, low, 0.0)))
        augmented[slot, :code_dim, cols] = block
        augmented[slot, code_dim:, cols] = extra.astype(BF16)

    for dc in range(1, n_c):
        forward(2, out_block, dc)
    for dc in range(n_c):
        rest(2, out_block, dc)

    def visit(k, carry):
        slot = k
        for part in range(n_c):
            kv_copy(slot, part, 1).wait_recv()
        absorb(slot, False)
        return carry

    lax.fori_loop(0, fr, visit, 0)

    for p in range(pairs):
        attended[:, p * LANES : (p + 1) * LANES] = (summed[p] / denom[p]).astype(BF16)

    def rows_at(slot):
        return pl.ds(pl.multiple_of(slot * rows, rows), rows)

    def exchange(dc, dh):
        c2, h2 = lax.rem(c + dc, n_c), lax.rem(h + dh, n_h)
        copy = pltpu.make_async_remote_copy(
            src_ref=attended.at[rows_at(c2 * n_h + h2)],
            dst_ref=gathered.at[g],
            send_sem=send_sems.at[len(started)],
            recv_sem=recv_sems.at[3, g],
            device_id=device(c2, h2),
            device_id_type=MESH,
        )
        copy.start()
        started.append(copy)

    order = [(dc, dh) for dc in range(n_c) for dh in range(n_h) if dc or dh]
    for dc, dh in reversed(order):
        exchange(dc, dh)

    def project_out(taken, slot, fresh):
        @pl.loop(0, width // tile)
        def _(n):
            cols = pl.ds(pl.multiple_of(n * tile, tile), tile)
            part = jnp.dot(taken, out_w[slot, :, cols], preferred_element_type=F32)
            if fresh:
                mixed[:, cols] = part
            else:
                mixed[:, cols] = mixed[:, cols] + part

    project_out(attended[rows_at(g), :], g, True)
    for dc, dh in order:
        slot = slot_of(dc, dh)
        arrived(3, lambda s: gathered.at[s], slot)
        project_out(gathered[slot], slot, False)

    encoded = (block_input[...].astype(F32) + mixed[...]).astype(BF16)
    encoded_ref[...] = encoded.reshape(fh, pos, width)
    latent = lax.dot_general(
        encoded, latent_w_ref[...], (((1,), (1,)), ((), ())), preferred_element_type=F32
    ).astype(BF16).astype(F32)
    square = jnp.sum(latent * latent, axis=1, keepdims=True)
    column = lax.broadcasted_iota(jnp.int32, lhs.shape, 1)
    lhs[...] = jnp.where(column < code_dim + 3, 1.0, 0.0)
    lhs[:, :code_dim] = -2.0 * latent
    left = lhs[...].astype(BF16)

    everyone = (pos, wanted_ref.shape[1])
    is_mine = lax.broadcasted_iota(jnp.int32, everyone, 0) + g * pos == lax.broadcasted_iota(
        jnp.int32, everyone, 1
    )
    for t in range(fh):
        mine = jnp.where(is_mine, jnp.broadcast_to(wanted_ref[t : t + 1, :], everyone), 0)
        wanted[t * pos : (t + 1) * pos, :] = jnp.broadcast_to(
            jnp.sum(mine, axis=1, keepdims=True), (pos, LANES)
        )
    lanes = lax.broadcasted_iota(jnp.int32, (1, LANES), 1)

    def search(step, state):
        least, chosen = state
        slot = step // (shard // c_tile)
        cols = pl.ds(pl.multiple_of((step % (shard // c_tile)) * c_tile, c_tile), c_tile)
        found = jnp.dot(left, augmented[slot, :, cols], preferred_element_type=F32)
        sought = wanted[...]
        for k in range(c_tile // LANES):
            part = found[:, k * LANES : (k + 1) * LANES]
            labels = lanes + (step * c_tile + k * LANES)
            least = jnp.minimum(least, part)
            chosen = jnp.where(sought == labels, part, chosen)
        return least, chosen

    least, chosen = lax.fori_loop(
        0, n_g * (shard // c_tile), search,
        (jnp.full((rows, LANES), 3e38, F32), jnp.zeros((rows, LANES), F32)),
    )
    least = (jnp.min(least, axis=1, keepdims=True) + square) / code_dim
    chosen = (jnp.sum(chosen, axis=1, keepdims=True) + square) / code_dim
    gap = chosen - least
    diagonal = lax.broadcasted_iota(jnp.int32, (pos, pos), 0) == lax.broadcasted_iota(
        jnp.int32, (pos, pos), 1
    )
    for t in range(fh):
        for ref, column in ((least_ref, least), (gap_ref, gap)):
            square_part = jnp.broadcast_to(column[t * pos : (t + 1) * pos], (pos, pos))
            ref[t : t + 1, :] = jnp.sum(
                jnp.where(diagonal, square_part, 0.0), axis=0, keepdims=True
            )

    for copy in started:
        copy.wait_send()

    @pl.when(fr + 1 < n_f)
    def _():
        halo.wait_send()

    for df in range(1, n_f):
        @pl.when(fr + df < n_f)
        def _():
            for part in range(n_c):
                kv_copy(fr, part, df).wait_send()


def shards(
    n_f, n_c, n_h,
    video, conv_weight, norm_gain, qkv_weight, out_weight, latent_weight, codebook, reference_codes,
):
    positions, frames_here, width = video.shape
    rows = positions * frames_here
    n_g = n_c * n_h
    slab = n_g * rows
    lw = qkv_weight.shape[2]
    pairs = lw // LANES
    code_dim, shard = codebook.shape
    sends = 3 * (n_c - 1 + n_h - 1 + (n_c - 1) * (n_h - 1)) + n_g - 1
    vmem = pl.BlockSpec(memory_space=pltpu.VMEM)
    hbm = pl.BlockSpec(memory_space=pltpu.HBM)
    encoded, least, gap = pl.pallas_call(
        functools.partial(encoder_kernel, n_f, n_c, n_h),
        out_shape=(
            jax.ShapeDtypeStruct((frames_here, positions, width), BF16),
            jax.ShapeDtypeStruct((frames_here, positions), F32),
            jax.ShapeDtypeStruct((frames_here, positions), F32),
        ),
        in_specs=[hbm] * 8,
        out_specs=(vmem, vmem, vmem),
        scratch_shapes=[
            pltpu.VMEM((1, width), F32),
            pltpu.VMEM((code_dim, width), BF16),
            pltpu.VMEM((frames_here, reference_codes.shape[0]), jnp.int32),
            pltpu.VMEM((2 + frames_here, positions, width), BF16),
            pltpu.VMEM(conv_weight.shape, BF16),
            pltpu.VMEM((rows, width), F32),
            pltpu.VMEM((rows, width), BF16),
            pltpu.VMEM((slab, width), BF16),
            pltpu.VMEM((3, width, lw), BF16),
            pltpu.VMEM((pairs, slab, LANES), BF16),
            pltpu.VMEM((n_f, n_c, 2, pairs, n_h * rows, LANES), BF16),
            pltpu.VMEM((pairs, slab, LANES), F32),
            pltpu.VMEM((pairs, slab, LANES), F32),
            pltpu.VMEM((pairs, slab, LANES), F32),
            pltpu.VMEM((slab, lw), BF16),
            pltpu.VMEM((n_g, rows, lw), BF16),
            pltpu.VMEM((n_g, lw, width), BF16),
            pltpu.VMEM((n_g, code_dim, shard), BF16),
            pltpu.VMEM((n_g, 2 * code_dim, shard), BF16),
            pltpu.VMEM((rows, 2 * code_dim), F32),
            pltpu.VMEM((rows, LANES), jnp.int32),
            pltpu.SemaphoreType.DMA((10,)),
            pltpu.SemaphoreType.DMA((sends,)),
            pltpu.SemaphoreType.DMA((4, n_g)),
            pltpu.SemaphoreType.DMA((n_f, n_c)),
            pltpu.SemaphoreType.DMA((n_f, n_c)),
            pltpu.SemaphoreType.DMA,
            pltpu.SemaphoreType.DMA,
        ],
        compiler_params=pltpu.CompilerParams(
            collective_id=0, has_side_effects=True, vmem_limit_bytes=48 * 1024 * 1024
        ),
    )(
        jnp.transpose(video, (1, 0, 2)),
        conv_weight,
        norm_gain.reshape(1, width),
        jnp.transpose(qkv_weight, (1, 0, 2)),
        out_weight,
        jnp.transpose(latent_weight),
        codebook,
        jnp.transpose(reference_codes),
    )
    return jnp.transpose(encoded, (1, 0, 2)), jnp.transpose(least), jnp.transpose(gap)


def solution(mesh):
    sizes = [mesh.shape[axis] for axis in ("frames", "code", "head")]
    return jax.shard_map(
        functools.partial(shards, *sizes),
        mesh=mesh,
        in_specs=(
            P(("code", "head"), ("groups", "frames"), None),
            P(),
            P(),
            P(None, None, ("code", "head")),
            P(("code", "head"), None),
            P(),
            P(None, ("code", "head")),
            P(None, ("groups", "frames")),
        ),
        out_specs=(
            P(("code", "head"), ("groups", "frames"), None),
            P(("code", "head"), ("groups", "frames")),
            P(("code", "head"), ("groups", "frames")),
        ),
        check_vma=False,
    )
```

```python
import functools
import math

import jax
import jax.numpy as jnp
from jax import lax
from jax.experimental import pallas as pl
from jax.experimental.pallas import tpu as pltpu
from jax.sharding import PartitionSpec as P

HEADS = 16
EPSILON = 1e-06
LANES = 128
MESH = pl.DeviceIdType.MESH
BF16 = jnp.bfloat16
F32 = jnp.float32


def tile_of(length, most):
    return math.gcd(length, most)


def encoder_kernel(
    n_f, n_c, n_h,
    video_hbm, conv_w_hbm, gain_hbm, qkv_w_hbm, out_w_hbm, latent_w_hbm, codes_hbm, wanted_hbm,
    encoded_ref, least_ref, gap_ref,
    gain_ref, latent_w_ref, wanted_ref, ext, conv_w, mixed, block_input, normed, qkv_w, queries, kv, top, denom, summed,
    attended, gathered, out_w, codes, augmented, lhs, wanted,
    local_sems, send_sems, recv_sems, kv_send, kv_recv, halo_send, halo_recv,
):
    n_g = n_c * n_h
    fr = lax.axis_index("frames")
    c = lax.axis_index("code")
    h = lax.axis_index("head")
    g = c * n_h + h
    fh, pos, width = video_hbm.shape
    rows = fh * pos
    chip_rows = n_h * rows
    lw = out_w_hbm.shape[0]
    pairs = lw // LANES
    head_dim = width // HEADS
    per_tile = LANES // head_dim
    slab = n_g * rows
    code_dim, shard = codes_hbm.shape

    def device(c2, h2):
        return {"code": c2, "head": h2}

    conv_copies = [
        pltpu.make_async_copy(conv_w_hbm.at[k], conv_w.at[k], local_sems.at[k]) for k in range(3)
    ]
    qkv_copy = pltpu.make_async_copy(qkv_w_hbm, qkv_w, local_sems.at[3])
    out_copy = pltpu.make_async_copy(out_w_hbm, out_w.at[g], local_sems.at[4])
    codes_copy = pltpu.make_async_copy(codes_hbm, codes.at[g], local_sems.at[5])
    video_copy = pltpu.make_async_copy(video_hbm, ext.at[pl.ds(2, fh)], local_sems.at[6])
    gain_copy = pltpu.make_async_copy(gain_hbm, gain_ref, local_sems.at[7])
    latent_w_copy = pltpu.make_async_copy(latent_w_hbm, latent_w_ref, local_sems.at[8])
    wanted_copy = pltpu.make_async_copy(wanted_hbm, wanted_ref, local_sems.at[9])
    small_copies = [gain_copy, latent_w_copy, wanted_copy]
    for copy in [codes_copy, video_copy] + conv_copies + [qkv_copy, out_copy] + small_copies:
        copy.start()

    barrier = pltpu.get_barrier_semaphore()
    for dc in range(n_c):
        for dh in range(n_h):
            if dc or dh:
                pl.semaphore_signal(
                    barrier, inc=1,
                    device_id=device(lax.rem(c + dc, n_c), lax.rem(h + dh, n_h)),
                    device_id_type=MESH,
                )
    for df in range(1, n_f):
        pl.semaphore_signal(
            barrier, inc=1, device_id={"frames": lax.rem(fr + df, n_f)}, device_id_type=MESH
        )
    pl.semaphore_wait(barrier, n_g - 1 + n_f - 1)

    halo = pltpu.make_async_remote_copy(
        src_ref=video_hbm.at[pl.ds(fh - 2, 2)],
        dst_ref=ext.at[pl.ds(0, 2)],
        send_sem=halo_send,
        recv_sem=halo_recv,
        device_id={"frames": lax.rem(fr + 1, n_f)},
        device_id_type=MESH,
    )

    @pl.when(fr + 1 < n_f)
    def _():
        halo.start()

    started = []

    def send(kind, block, slot, c2, h2):
        copy = pltpu.make_async_remote_copy(
            src_ref=block(slot),
            dst_ref=block(slot),
            send_sem=send_sems.at[len(started)],
            recv_sem=recv_sems.at[kind, slot],
            device_id=device(c2, h2),
            device_id_type=MESH,
        )
        copy.start()
        started.append(copy)

    def arrived(kind, block, slot):
        pltpu.make_async_remote_copy(
            src_ref=block(slot),
            dst_ref=block(slot),
            send_sem=send_sems.at[0],
            recv_sem=recv_sems.at[kind, slot],
            device_id=device(c, lax.rem(h + 1, n_h)),
            device_id_type=MESH,
        ).wait_recv()

    def slot_of(dc, dh):
        return lax.rem(c + n_c - dc, n_c) * n_h + lax.rem(h + n_h - dh, n_h)

    def spread(kind, block):
        for dc in range(1, n_c):
            send(kind, block, g, lax.rem(c + dc, n_c), h)
        for dh in range(1, n_h):
            send(kind, block, g, c, lax.rem(h + dh, n_h))

    def forward(kind, block, dc):
        slot = slot_of(dc, 0)
        arrived(kind, block, slot)
        for dh in range(1, n_h):
            send(kind, block, slot, c, lax.rem(h + dh, n_h))

    def rest(kind, block, dc):
        for dh in range(1, n_h):
            arrived(kind, block, slot_of(dc, dh))

    def codes_block(slot):
        return codes.at[slot]

    def normed_block(slot):
        return normed.at[pl.ds(pl.multiple_of(slot * rows, rows), rows)]

    def out_block(slot):
        return out_w.at[slot]

    codes_copy.wait()
    spread(0, codes_block)

    video_copy.wait()
    tile = tile_of(width, 1024)

    def tap(k):
        conv_copies[k].wait()
        taken = ext[2 - k : 2 - k + fh].reshape(rows, width)

        @pl.loop(0, width // tile)
        def _(n):
            cols = pl.ds(pl.multiple_of(n * tile, tile), tile)
            part = jnp.dot(taken, conv_w[k, :, cols], preferred_element_type=F32)
            if k == 0:
                mixed[:, cols] = part
            else:
                mixed[:, cols] = mixed[:, cols] + part

    tap(0)

    @pl.when(fr > 0)
    def _():
        halo.wait_recv()

    @pl.when(fr == 0)
    def _():
        ext[:2] = jnp.zeros((2, pos, width), BF16)

    tap(1)
    tap(2)
    for copy in small_copies:
        copy.wait()
    conv = mixed[...]
    values = (ext[2:].reshape(rows, width).astype(F32) + conv / (1.0 + jnp.exp(-conv))).astype(BF16)
    block_input[...] = values
    values32 = values.astype(F32)
    mean_square = jnp.mean(values32 * values32, axis=-1, keepdims=True)
    normed[pl.ds(pl.multiple_of(g * rows, rows), rows), :] = (
        values32 * lax.rsqrt(mean_square + EPSILON) * gain_ref[...]
    ).astype(BF16)
    spread(1, normed_block)

    def project(c2):
        at = pl.ds(pl.multiple_of(c2 * chip_rows, chip_rows), chip_rows)
        taken = normed[at, :]
        for kind in range(3):
            out = jnp.dot(taken, qkv_w[kind], preferred_element_type=F32)
            out = out.astype(BF16)
            for p in range(pairs):
                piece = out[:, p * LANES : (p + 1) * LANES]
                if kind == 0:
                    queries[p, at, :] = piece * (1.0 / math.sqrt(head_dim))
                else:
                    kv[fr, c2, kind - 1, p] = piece

    def kv_copy(slot, c2, df):
        return pltpu.make_async_remote_copy(
            src_ref=kv.at[slot, c2],
            dst_ref=kv.at[slot, c2],
            send_sem=kv_send.at[df, c2],
            recv_sem=kv_recv.at[slot, c2],
            device_id={"frames": lax.rem(fr + df, n_f)},
            device_id_type=MESH,
        )

    def send_kv(c2):
        for df in reversed(range(1, n_f)):
            @pl.when(fr + df < n_f)
            def _():
                kv_copy(fr, c2, df).start()

    qkv_copy.wait()
    rest(1, normed_block, 0)
    project(c)
    send_kv(c)
    for dc in range(1, n_c):
        forward(1, normed_block, dc)
    out_copy.wait()
    spread(2, out_block)
    for dc in range(1, n_c):
        rest(1, normed_block, dc)
        other = lax.rem(c + n_c - dc, n_c)
        project(other)
        send_kv(other)

    q_tile = tile_of(slab, 256)
    lane = lax.broadcasted_iota(jnp.int32, (q_tile, LANES), 1) // head_dim

    def by_head(parts):
        out = parts[0]
        for k in range(1, per_tile):
            out = jnp.where(lane == k, parts[k], out)
        return out

    def absorb(slot, own):
        @pl.loop(0, pairs * (slab // q_tile))
        def _(step):
            p = step // (slab // q_tile)
            first = (step % (slab // q_tile)) * q_tile
            at = pl.ds(pl.multiple_of(first, q_tile), q_tile)
            q = queries[p, at, :]
            k = kv[slot, :, 0, p].reshape(slab, LANES)
            v = kv[slot, :, 1, p].reshape(slab, LANES)
            if own:
                q_row = first + lax.broadcasted_iota(jnp.int32, (q_tile, slab), 0)
                k_row = lax.broadcasted_iota(jnp.int32, (q_tile, slab), 1)
                allowed = (k_row // pos) % fh <= (q_row // pos) % fh
            else:
                old_top = top[p, at, :]
            tops, factors, sums, outs = [], [], [], []
            for hh in range(per_tile):
                mine = jnp.where(lane == hh, q, jnp.zeros_like(q))
                scores = lax.dot_general(mine, k, (((1,), (1,)), ((), ())), preferred_element_type=F32)
                if own:
                    scores = jnp.where(allowed, scores, -1e30)
                fresh = jnp.max(scores, axis=1, keepdims=True)
                if not own:
                    old = old_top[:, hh * head_dim : hh * head_dim + 1]
                    fresh = jnp.maximum(fresh, old)
                    factors.append(jnp.exp(old - fresh))
                weights = jnp.exp(scores - fresh)
                tops.append(fresh)
                sums.append(jnp.sum(weights, axis=1, keepdims=True))
                outs.append(jnp.dot(weights.astype(BF16), v, preferred_element_type=F32))
            top[p, at, :] = by_head([jnp.broadcast_to(x, (q_tile, LANES)) for x in tops])
            total = by_head([jnp.broadcast_to(x, (q_tile, LANES)) for x in sums])
            out = by_head(outs)
            if own:
                denom[p, at, :] = total
                summed[p, at, :] = out
            else:
                factor = by_head([jnp.broadcast_to(x, (q_tile, LANES)) for x in factors])
                denom[p, at, :] = denom[p, at, :] * factor + total
                summed[p, at, :] = summed[p, at, :] * factor + out

    absorb(fr, True)

    for dc in range(1, n_c):
        forward(0, codes_block, dc)
    for dc in range(n_c):
        rest(0, codes_block, dc)
    c_tile = tile_of(shard, 8192)

    @pl.loop(0, n_g * (shard // c_tile))
    def _(step):
        slot = step // (shard // c_tile)
        cols = pl.ds(pl.multiple_of((step % (shard // c_tile)) * c_tile, c_tile), c_tile)
        block = codes[slot, :, cols]
        block32 = block.astype(F32)
        squares = jnp.sum(block32 * block32, axis=0, keepdims=True)
        high = squares.astype(BF16).astype(F32)
        middle = (squares - high).astype(BF16).astype(F32)
        low = squares - high - middle
        row = lax.broadcasted_iota(jnp.int32, (code_dim, c_tile), 0)
        extra = jnp.where(row == 0, high, jnp.where(row == 1, middle, jnp.where(row == 2, low, 0.0)))
        augmented[slot, :code_dim, cols] = block
        augmented[slot, code_dim:, cols] = extra.astype(BF16)

    for dc in range(1, n_c):
        forward(2, out_block, dc)
    for dc in range(n_c):
        rest(2, out_block, dc)

    def visit(k, carry):
        slot = k
        for part in range(n_c):
            kv_copy(slot, part, 1).wait_recv()
        absorb(slot, False)
        return carry

    lax.fori_loop(0, fr, visit, 0)

    for p in range(pairs):
        attended[:, p * LANES : (p + 1) * LANES] = (summed[p] / denom[p]).astype(BF16)

    def rows_at(slot):
        return pl.ds(pl.multiple_of(slot * rows, rows), rows)

    def exchange(dc, dh):
        c2, h2 = lax.rem(c + dc, n_c), lax.rem(h + dh, n_h)
        copy = pltpu.make_async_remote_copy(
            src_ref=attended.at[rows_at(c2 * n_h + h2)],
            dst_ref=gathered.at[g],
            send_sem=send_sems.at[len(started)],
            recv_sem=recv_sems.at[3, g],
            device_id=device(c2, h2),
            device_id_type=MESH,
        )
        copy.start()
        started.append(copy)

    order = [(dc, dh) for dc in range(n_c) for dh in range(n_h) if dc or dh]
    for dc, dh in reversed(order):
        exchange(dc, dh)

    def project_out(taken, slot, fresh):
        @pl.loop(0, width // tile)
        def _(n):
            cols = pl.ds(pl.multiple_of(n * tile, tile), tile)
            part = jnp.dot(taken, out_w[slot, :, cols], preferred_element_type=F32)
            if fresh:
                mixed[:, cols] = part
            else:
                mixed[:, cols] = mixed[:, cols] + part

    project_out(attended[rows_at(g), :], g, True)
    for dc, dh in order:
        slot = slot_of(dc, dh)
        arrived(3, lambda s: gathered.at[s], slot)
        project_out(gathered[slot], slot, False)

    encoded = (block_input[...].astype(F32) + mixed[...]).astype(BF16)
    encoded_ref[...] = encoded.reshape(fh, pos, width)
    latent = lax.dot_general(
        encoded, latent_w_ref[...], (((1,), (1,)), ((), ())), preferred_element_type=F32
    ).astype(BF16).astype(F32)
    square = jnp.sum(latent * latent, axis=1, keepdims=True)
    column = lax.broadcasted_iota(jnp.int32, lhs.shape, 1)
    lhs[...] = jnp.where(column < code_dim + 3, 1.0, 0.0)
    lhs[:, :code_dim] = -2.0 * latent
    left = lhs[...].astype(BF16)

    everyone = (pos, wanted_ref.shape[1])
    is_mine = lax.broadcasted_iota(jnp.int32, everyone, 0) + g * pos == lax.broadcasted_iota(
        jnp.int32, everyone, 1
    )
    for t in range(fh):
        mine = jnp.where(is_mine, jnp.broadcast_to(wanted_ref[t : t + 1, :], everyone), 0)
        wanted[t * pos : (t + 1) * pos, :] = jnp.broadcast_to(
            jnp.sum(mine, axis=1, keepdims=True), (pos, LANES)
        )
    lanes = lax.broadcasted_iota(jnp.int32, (1, LANES), 1)

    def search(step, state):
        least, chosen = state
        slot = step // (shard // c_tile)
        cols = pl.ds(pl.multiple_of((step % (shard // c_tile)) * c_tile, c_tile), c_tile)
        found = jnp.dot(left, augmented[slot, :, cols], preferred_element_type=F32)
        sought = wanted[...]
        for k in range(c_tile // LANES):
            part = found[:, k * LANES : (k + 1) * LANES]
            labels = lanes + (step * c_tile + k * LANES)
            least = jnp.minimum(least, part)
            chosen = jnp.where(sought == labels, part, chosen)
        return least, chosen

    least, chosen = lax.fori_loop(
        0, n_g * (shard // c_tile), search,
        (jnp.full((rows, LANES), 3e38, F32), jnp.zeros((rows, LANES), F32)),
    )
    least = (jnp.min(least, axis=1, keepdims=True) + square) / code_dim
    chosen = (jnp.sum(chosen, axis=1, keepdims=True) + square) / code_dim
    gap = chosen - least
    diagonal = lax.broadcasted_iota(jnp.int32, (pos, pos), 0) == lax.broadcasted_iota(
        jnp.int32, (pos, pos), 1
    )
    for t in range(fh):
        for ref, column in ((least_ref, least), (gap_ref, gap)):
            square_part = jnp.broadcast_to(column[t * pos : (t + 1) * pos], (pos, pos))
            ref[t : t + 1, :] = jnp.sum(
                jnp.where(diagonal, square_part, 0.0), axis=0, keepdims=True
            )

    for copy in started:
        copy.wait_send()

    @pl.when(fr + 1 < n_f)
    def _():
        halo.wait_send()

    for df in range(1, n_f):
        @pl.when(fr + df < n_f)
        def _():
            for part in range(n_c):
                kv_copy(fr, part, df).wait_send()


def shards(
    n_f, n_c, n_h,
    video, conv_weight, norm_gain, qkv_weight, out_weight, latent_weight, codebook, reference_codes,
):
    positions, frames_here, width = video.shape
    rows = positions * frames_here
    n_g = n_c * n_h
    slab = n_g * rows
    lw = qkv_weight.shape[2]
    pairs = lw // LANES
    code_dim, shard = codebook.shape
    sends = 3 * (n_c - 1 + n_h - 1 + (n_c - 1) * (n_h - 1)) + n_g - 1
    vmem = pl.BlockSpec(memory_space=pltpu.VMEM)
    hbm = pl.BlockSpec(memory_space=pltpu.HBM)
    encoded, least, gap = pl.pallas_call(
        functools.partial(encoder_kernel, n_f, n_c, n_h),
        out_shape=(
            jax.ShapeDtypeStruct((frames_here, positions, width), BF16),
            jax.ShapeDtypeStruct((frames_here, positions), F32),
            jax.ShapeDtypeStruct((frames_here, positions), F32),
        ),
        in_specs=[hbm] * 8,
        out_specs=(vmem, vmem, vmem),
        scratch_shapes=[
            pltpu.VMEM((1, width), F32),
            pltpu.VMEM((code_dim, width), BF16),
            pltpu.VMEM((frames_here, reference_codes.shape[0]), jnp.int32),
            pltpu.VMEM((2 + frames_here, positions, width), BF16),
            pltpu.VMEM(conv_weight.shape, BF16),
            pltpu.VMEM((rows, width), F32),
            pltpu.VMEM((rows, width), BF16),
            pltpu.VMEM((slab, width), BF16),
            pltpu.VMEM((3, width, lw), BF16),
            pltpu.VMEM((pairs, slab, LANES), BF16),
            pltpu.VMEM((n_f, n_c, 2, pairs, n_h * rows, LANES), BF16),
            pltpu.VMEM((pairs, slab, LANES), F32),
            pltpu.VMEM((pairs, slab, LANES), F32),
            pltpu.VMEM((pairs, slab, LANES), F32),
            pltpu.VMEM((slab, lw), BF16),
            pltpu.VMEM((n_g, rows, lw), BF16),
            pltpu.VMEM((n_g, lw, width), BF16),
            pltpu.VMEM((n_g, code_dim, shard), BF16),
            pltpu.VMEM((n_g, 2 * code_dim, shard), BF16),
            pltpu.VMEM((rows, 2 * code_dim), F32),
            pltpu.VMEM((rows, LANES), jnp.int32),
            pltpu.SemaphoreType.DMA((10,)),
            pltpu.SemaphoreType.DMA((sends,)),
            pltpu.SemaphoreType.DMA((4, n_g)),
            pltpu.SemaphoreType.DMA((n_f, n_c)),
            pltpu.SemaphoreType.DMA((n_f, n_c)),
            pltpu.SemaphoreType.DMA,
            pltpu.SemaphoreType.DMA,
        ],
        compiler_params=pltpu.CompilerParams(
            collective_id=0, has_side_effects=True, vmem_limit_bytes=60 * 1024 * 1024
        ),
    )(
        jnp.transpose(video, (1, 0, 2)),
        conv_weight,
        norm_gain.reshape(1, width),
        jnp.transpose(qkv_weight, (1, 0, 2)),
        out_weight,
        jnp.transpose(latent_weight),
        codebook,
        jnp.transpose(reference_codes),
    )
    return jnp.transpose(encoded, (1, 0, 2)), jnp.transpose(least), jnp.transpose(gap)


def solution(mesh):
    sizes = [mesh.shape[axis] for axis in ("frames", "code", "head")]
    return jax.shard_map(
        functools.partial(shards, *sizes),
        mesh=mesh,
        in_specs=(
            P(("code", "head"), ("groups", "frames"), None),
            P(),
            P(),
            P(None, None, ("code", "head")),
            P(("code", "head"), None),
            P(),
            P(None, ("code", "head")),
            P(None, ("groups", "frames")),
        ),
        out_specs=(
            P(("code", "head"), ("groups", "frames"), None),
            P(("code", "head"), ("groups", "frames")),
            P(("code", "head"), ("groups", "frames")),
        ),
        check_vma=False,
    )
```
